32 devices in a mesh: half: 2 (over y), row: 4 (over x, core), col: 4 (over z).
Axes of the slice: x: 2, y: 2, z: 4, core: 2. Of those that a mesh axis runs over, the one named last changes fastest.
Arguments:
- front: bfloat16 [2, 16384, 16384], P('half', 'row', 'col'), may hold values from -6 to 6, as said below
- panel: bfloat16 [2, 16384, 1024], P('half', 'row', 'col'), may hold values from -2.5 to 2.5
- inverse_block: bfloat16 [2, 1024, 1024], P('half', None, 'col'), as said below
- child_maps: int32 [2, 16384], replicated, may hold values from 0 to 16383, as said below
- root_front: bfloat16 [16384, 16384], P(('half', 'row'), 'col'), may hold values from -6 to 6, as said below
Outputs:
- root_sum: float32 [16384, 16384], P(('half', 'row'), 'col')
The draws below stay inside these ranges and needn't reach their ends.
Inputs may be any that keep to these rules, and one draw needn't show every extreme that they name: `child_maps`: each row is a permutation of the 16384 root indices. For each child, in every aligned block of 4096 positions, the k-th aligned run of 512 positions maps into the k-th aligned block of 2048 root indices. `inverse_block`: each matrix is lower triangular with a positive diagonal. `front`: each child's matrix is symmetric. `root_front`: the matrix is symmetric.
All inputs are finite; a program needn't handle non-finite values.
Results may differ from the reference program's by a relative error of at most 0.0041.
Values may be sent and summed in bfloat16 or wider, within the bound.
A program may use at most 256 MiB of HBM per device.

```python
import jax
import jax.numpy as jnp

S = 16384
P_SIZE = 1024
CHILD_BLOCK = 4096
ROOT_BLOCK = 2048
SHARE = 512


def symmetric_field(key, shape):
    base = jax.random.normal(key, shape, jnp.float32)
    mixed = (base + jnp.swapaxes(base, -1, -2)) * 0.70710678
    return jnp.clip(mixed, -6.0, 6.0)


def draw_front(key, part):
    key = jax.random.fold_in(key, 23)
    return symmetric_field(key, (2, S, S)).astype(jnp.bfloat16)


def draw_root_front(key, part):
    key = jax.random.fold_in(key, 31)
    return symmetric_field(key, (S, S)).astype(jnp.bfloat16)


def draw_inverse_block(key, part):
    key = jax.random.fold_in(key, 11)
    first_key, second_key = jax.random.split(key)
    spread = jax.random.normal(first_key, (2, P_SIZE, P_SIZE), jnp.float32) * (0.6 / P_SIZE ** 0.5)
    diagonal = jnp.exp(jax.random.uniform(second_key, (2, P_SIZE), jnp.float32, -0.7, 0.7))
    matrix = jnp.tril(spread, -1) + diagonal[:, :, None] * jnp.eye(P_SIZE, dtype=jnp.float32)[None]
    return matrix.astype(jnp.bfloat16)


def one_map(key):
    groups = CHILD_BLOCK // SHARE
    blocks = S // CHILD_BLOCK
    within = jax.vmap(lambda subkey: jax.random.permutation(subkey, ROOT_BLOCK))(jax.random.split(key, groups))
    position = jnp.arange(CHILD_BLOCK, dtype=jnp.int32)[None, :]
    target = jnp.broadcast_to(position // SHARE, (blocks, CHILD_BLOCK))
    member = jnp.arange(blocks, dtype=jnp.int32)[:, None] * SHARE + position % SHARE
    return (target * ROOT_BLOCK + within[target, member]).reshape(-1).astype(jnp.int32)


def draw_child_maps(key, part):
    key = jax.random.fold_in(key, 5)
    return jnp.stack([one_map(jax.random.fold_in(key, 0)), one_map(jax.random.fold_in(key, 1))])


def shard_levels(rng, dims, cuts, least, high):
    gain, own = 1.0, jax.random.fold_in(rng, 6)
    for dim, parts in cuts:
        steps = jnp.exp(jax.random.uniform(jax.random.fold_in(own, dim), (parts,), jnp.float32, least / len(cuts), high / len(cuts)))
        gain = gain * jnp.repeat(steps, dims[dim] // parts).reshape([-1 if axis == dim else 1 for axis in range(len(dims))])
    return gain


def centred(key, shape, width, most, shards=(), kind=jnp.bfloat16):
    values = width * jax.random.normal(key, shape, jnp.float32)
    if shards:
        values = values * shard_levels(key, shape, shards, -0.22, 0.18)
    return jnp.clip(values, -most, most).astype(kind)


def setup_inputs(seed: int = 0) -> dict:
    key_list = jax.random.split(jax.random.key(seed), 6)
    front = draw_front(jax.random.fold_in(key_list[5], 71), 0)
    panel = centred(key_list[1], (2, S, P_SIZE), 0.18, 2.5, ((0, 2), (1, 4), (2, 4)))
    inverse_block = draw_inverse_block(jax.random.fold_in(key_list[5], 71), 0)
    child_maps = draw_child_maps(jax.random.fold_in(key_list[5], 71), 0)
    root_front = draw_root_front(jax.random.fold_in(key_list[5], 71), 0)
    return {"front": front, "panel": panel, "inverse_block": inverse_block, "child_maps": child_maps, "root_front": root_front}


def reference(front, panel, inverse_block, child_maps, root_front):
    root_sum = root_front.astype(jnp.float32)
    for child_idx in range(2):
        lower_panel = jnp.dot(panel[child_idx], inverse_block[child_idx].T, preferred_element_type=jnp.float32).astype(jnp.bfloat16)
        product = jnp.dot(lower_panel, lower_panel.T, preferred_element_type=jnp.float32)
        schur_block = (front[child_idx].astype(jnp.float32) - product).astype(jnp.bfloat16)
        inverse_map = jnp.zeros((S,), jnp.int32).at[child_maps[child_idx]].set(jnp.arange(S, dtype=jnp.int32))
        placed = jnp.take(jnp.take(schur_block, inverse_map, axis=0), inverse_map, axis=1)
        root_sum = root_sum + placed.astype(jnp.float32)
    row_ids = jnp.arange(S, dtype=jnp.int32)[:, None]
    col_ids = jnp.arange(S, dtype=jnp.int32)[None, :]
    return jnp.where(row_ids >= col_ids, root_sum, jnp.zeros_like(root_sum))
```

```python
import functools

import jax
import jax.numpy as jnp
from jax import lax
from jax.experimental import pallas as pl
from jax.experimental.pallas import tpu as pltpu
from jax.sharding import PartitionSpec as P

MESH = pl.DeviceIdType.MESH


def contract(left, right):
    return lax.dot_general(
        left, right, (((1,), (1,)), ((), ())), preferred_element_type=jnp.float32
    )


def column_factor(lower, n):
    axes = ("row", "col")
    row_idx = lax.axis_index("row")
    col_idx = lax.axis_index("col")
    half_rows = lower.shape[0] // 2
    top, bottom = lower[:half_rows], lower[half_rows:]
    partner = lax.ppermute(lower, axes, [(c * n + c, (c ^ 1) * n + c) for c in range(n)])
    part = None
    for k in range(1, n // 2):
        evens, odds = [], []
        for c in range(n):
            far = 2 * ((c // 2 + k) % (n // 2))
            evens.append((c * n + c, far * n + c))
            odds.append((c * n + c, (far + 1) * n + c))
        got_even = lax.ppermute(top, axes, evens)
        got_odd = lax.ppermute(bottom, axes, odds)
        got = jnp.where(row_idx % 2 == 0, got_even, got_odd)
        part = got if part is None else part + got
    other = lax.ppermute(part, "row", [(r, r ^ 1) for r in range(n)])
    even = row_idx % 2 == 0
    joined = jnp.concatenate(
        [jnp.where(even, part, other), jnp.where(even, other, part)], axis=0
    )
    near = jnp.where(row_idx == col_idx, lower, partner)
    return jnp.where(row_idx // 2 == col_idx // 2, near, joined)


def exchange_kernel(n, schur, arr_a, arr_b, send_sem, recv_sem, local_sem):
    total = 2 * n * n
    h = lax.axis_index("half")
    r = lax.axis_index("row")
    z = lax.axis_index("col")
    me = (h * n + r) * n + z
    rs = arr_a.shape[3]
    cs = arr_a.shape[4]

    def place(index):
        return index // (n * n), (index // n) % n, index % n

    barrier = pltpu.get_barrier_semaphore()

    @pl.loop(1, total)
    def _(step):
        ph, pr, pz = place(lax.rem(me + step, total))
        pl.semaphore_signal(barrier, inc=1, device_id=(ph, pr, pz), device_id_type=MESH)

    pl.semaphore_wait(barrier, total - 1)

    def visit(step, act):
        ph, pr, pz = place(lax.rem(me + step, total))
        t = ph * n + pr
        near = jnp.abs(z - pz)
        far = jnp.abs(r - pz)
        row_at = pl.multiple_of(t * rs, rs)
        col_at = pl.multiple_of(pz * cs, cs)

        def remote(src, dst, kind):
            act(
                pltpu.make_async_remote_copy(
                    src_ref=src,
                    dst_ref=dst,
                    send_sem=send_sem.at[step, kind],
                    recv_sem=recv_sem.at[h, r, z] if kind == 0 else recv_sem.at[h, z, r],
                    device_id=(ph, pr, pz),
                    device_id_type=MESH,
                )
            )

        for width, fits in ((cs, t > 2 * pz), (rs, t == 2 * pz)):

            @pl.when(fits & (near <= far))
            def _():
                remote(
                    schur.at[pl.ds(row_at, rs), pl.ds(col_at, width)],
                    arr_a.at[h, r, z, :, pl.ds(0, width)],
                    0,
                )

            @pl.when(fits & (near < far))
            def _():
                remote(
                    schur.at[pl.ds(col_at, width), pl.ds(row_at, rs)],
                    arr_b.at[h, z, r, pl.ds(0, width), :],
                    1,
                )

    @pl.loop(1, total)
    def _(step):
        visit(step, lambda copy: copy.start())

    my_t = h * n + r
    row_at = pl.multiple_of(my_t * rs, rs)
    col_at = pl.multiple_of(z * cs, cs)
    own_a = pltpu.make_async_copy(
        schur.at[pl.ds(row_at, rs), pl.ds(col_at, cs)], arr_a.at[h, r, z], local_sem.at[0]
    )
    own_b = pltpu.make_async_copy(
        schur.at[pl.ds(col_at, cs), pl.ds(row_at, rs)], arr_b.at[h, z, r], local_sem.at[1]
    )
    own_a.start()
    own_b.start()
    own_a.wait()
    own_b.wait()

    @pl.loop(1, total)
    def _(step):
        visit(step, lambda copy: copy.wait_send())

    @pl.loop(1, total)
    def _(step):
        sh, sr, sz = place(lax.rem(me + total - step, total))
        near = jnp.abs(sz - z)
        far = jnp.abs(sr - z)
        for width, fits in ((cs, my_t > 2 * z), (rs, my_t == 2 * z)):

            @pl.when(fits & (near <= far))
            def _():
                dst = arr_a.at[sh, sr, sz, :, pl.ds(0, width)]
                pltpu.make_async_copy(dst, dst, recv_sem.at[sh, sr, sz]).wait()

            @pl.when(fits & (near < far))
            def _():
                dst = arr_b.at[sh, sz, sr, pl.ds(0, width), :]
                pltpu.make_async_copy(dst, dst, recv_sem.at[sh, sz, sr]).wait()


def exchange(schur, n):
    rs = schur.shape[0] // (2 * n)
    cs = 2 * rs
    return pl.pallas_call(
        functools.partial(exchange_kernel, n),
        out_shape=(
            jax.ShapeDtypeStruct((2, n, n, rs, cs), schur.dtype),
            jax.ShapeDtypeStruct((2, n, n, cs, rs), schur.dtype),
        ),
        in_specs=[pl.BlockSpec(memory_space=pl.ANY)],
        out_specs=(pl.BlockSpec(memory_space=pl.ANY), pl.BlockSpec(memory_space=pl.ANY)),
        scratch_shapes=[
            pltpu.SemaphoreType.DMA((2 * n * n, 2)),
            pltpu.SemaphoreType.DMA((2, n, n)),
            pltpu.SemaphoreType.DMA((2,)),
        ],
        compiler_params=pltpu.CompilerParams(collective_id=0, has_side_effects=True),
    )(schur)


def assemble_kernel(n, row_map, col_map, arr_a, arr_b, root, out, square, rowed, sems):
    q = pl.program_id(0)
    j = pl.program_id(1)
    h_idx = lax.axis_index("half")
    r_idx = lax.axis_index("row")
    c_idx = lax.axis_index("col")
    t = h_idx * n + r_idx
    block = square.shape[1]
    rs = block // n
    tile = min(256, block)
    width = out.shape[1]
    needed = t >= 2 * c_idx + q

    def tiles(h, act):
        for b in range(n):
            for c in range(n):
                straight = jnp.abs(c - c_idx) <= jnp.abs(b - c_idx)
                dst = square.at[h, pl.ds(b * rs, rs), pl.ds(c * rs, rs)]
                act(b, c, straight, dst)

    @pl.when(needed & (j == 0))
    def _():
        def start(h, b, c, straight, dst):
            at = pl.multiple_of(q * rs, rs)

            @pl.when(straight)
            def _():
                pltpu.make_async_copy(
                    arr_a.at[h, b, c, :, pl.ds(at, rs)], dst, sems.at[h, b, c]
                ).start()

            @pl.when(jnp.logical_not(straight))
            def _():
                pltpu.make_async_copy(
                    arr_b.at[h, b, c, pl.ds(at, rs), :], dst, sems.at[h, b, c]
                ).start()

        def finish(h, b, c, straight, dst):
            pltpu.make_async_copy(
                arr_a.at[h, b, c, :, pl.ds(0, rs)], dst, sems.at[h, b, c]
            ).wait()

            @pl.when(jnp.logical_not(straight))
            def _():
                eye = (
                    lax.broadcasted_iota(jnp.int32, (rs, rs), 0)
                    == lax.broadcasted_iota(jnp.int32, (rs, rs), 1)
                ).astype(jnp.bfloat16)
                dst[...] = contract(eye, dst[...]).astype(jnp.bfloat16)

        for h in range(2):
            tiles(h, functools.partial(start, h))
        for h in range(2):
            tiles(h, functools.partial(finish, h))

            @pl.loop(0, block // tile)
            def _(i):
                at = pl.multiple_of(i * tile, tile)
                pick = (
                    lax.broadcasted_iota(jnp.int32, (tile, block), 0) + at
                    == row_map[h : h + 1, :]
                ).astype(jnp.bfloat16)
                rowed[h, pl.ds(at, tile), :] = jnp.dot(
                    pick, square[h], preferred_element_type=jnp.float32
                ).astype(jnp.bfloat16)

    @pl.when(needed)
    def _():
        ids = lax.broadcasted_iota(jnp.int32, (block, width), 1) + j * width
        picks = [
            (col_map[0, h, :, :] == ids).astype(jnp.bfloat16) for h in range(2)
        ]
        first_row = t * block
        first_col = (2 * c_idx + q) * block + j * width
        for i in range(block // tile):
            rows = pl.ds(i * tile, tile)
            value = root[rows, :].astype(jnp.float32)
            for h in range(2):
                value = value + jnp.dot(
                    rowed[h, rows, :], picks[h], preferred_element_type=jnp.float32
                )
            row_ids = lax.broadcasted_iota(jnp.int32, (tile, width), 0) + (
                first_row + i * tile
            )
            col_ids = lax.broadcasted_iota(jnp.int32, (tile, width), 1) + first_col
            out[rows, :] = jnp.where(row_ids >= col_ids, value, 0.0)

    @pl.when(jnp.logical_not(needed))
    def _():
        out[...] = jnp.zeros_like(out)


def assemble(row_map, col_map, arr_a, arr_b, root_front, n):
    block = root_front.shape[0]
    width = min(256, block)
    steps = block // width
    return pl.pallas_call(
        functools.partial(assemble_kernel, n),
        grid=(2, steps),
        out_shape=jax.ShapeDtypeStruct(root_front.shape, jnp.float32),
        in_specs=[
            pl.BlockSpec((2, block), lambda q, j: (0, 0)),
            pl.BlockSpec((1, 2, block, 1), lambda q, j: (q, 0, 0, 0)),
            pl.BlockSpec(memory_space=pl.ANY),
            pl.BlockSpec(memory_space=pl.ANY),
            pl.BlockSpec((block, width), lambda q, j: (0, q * steps + j)),
        ],
        out_specs=pl.BlockSpec((block, width), lambda q, j: (0, q * steps + j)),
        scratch_shapes=[
            pltpu.VMEM((2, block, block), jnp.bfloat16),
            pltpu.VMEM((2, block, block), jnp.bfloat16),
            pltpu.SemaphoreType.DMA((2, n, n)),
        ],
        compiler_params=pltpu.CompilerParams(vmem_limit_bytes=58 * 1024 * 1024),
    )(row_map, col_map, arr_a, arr_b, root_front)


def body(front, panel, inverse_block, child_maps, root_front):
    n = lax.axis_size("row")
    halves = lax.axis_size("half")
    target = lax.axis_index("half") * n + lax.axis_index("row")
    col_idx = lax.axis_index("col")
    block_front = front[0]
    span = block_front.shape[0]
    share = span // (halves * n)
    block = root_front.shape[0]

    full_panel = lax.all_gather(panel[0], "col", axis=1, tiled=True)
    full_inverse = lax.all_gather(inverse_block[0], "col", axis=1, tiled=True)
    lower_rows = contract(full_panel, full_inverse).astype(jnp.bfloat16)
    lower_cols = column_factor(lower_rows, n)
    update = contract(lower_rows, lower_cols)
    schur_block = (block_front.astype(jnp.float32) - update).astype(jnp.bfloat16)
    arr_a, arr_b = exchange(schur_block, n)

    runs = child_maps.reshape(halves, n, halves * n, share)

    def local_ids(run):
        picked = lax.dynamic_index_in_dim(runs, run, axis=2, keepdims=False)
        return picked.reshape(halves, n * share) - run * block

    row_map = local_ids(target)
    col_map = jnp.stack([local_ids(2 * col_idx), local_ids(2 * col_idx + 1)])
    return assemble(row_map, col_map[..., None], arr_a, arr_b, root_front, n)


def solution(mesh):
    return jax.shard_map(
        body,
        mesh=mesh,
        in_specs=(
            P("half", "row", "col"),
            P("half", "row", "col"),
            P("half", None, "col"),
            P(),
            P(("half", "row"), "col"),
        ),
        out_specs=P(("half", "row"), "col"),
        check_vma=False,
    )
```

```python
import functools

import jax
import jax.numpy as jnp
from jax import lax
from jax.experimental import pallas as pl
from jax.experimental.pallas import tpu as pltpu
from jax.sharding import PartitionSpec as P

MESH = pl.DeviceIdType.MESH


def contract(left, right):
    return lax.dot_general(
        left, right, (((1,), (1,)), ((), ())), preferred_element_type=jnp.float32
    )


def column_factor(lower, n):
    axes = ("row", "col")
    row_idx = lax.axis_index("row")
    col_idx = lax.axis_index("col")
    half_rows = lower.shape[0] // 2
    top, bottom = lower[:half_rows], lower[half_rows:]
    partner = lax.ppermute(lower, axes, [(c * n + c, (c ^ 1) * n + c) for c in range(n)])
    part = None
    for k in range(1, n // 2):
        evens, odds = [], []
        for c in range(n):
            far = 2 * ((c // 2 + k) % (n // 2))
            evens.append((c * n + c, far * n + c))
            odds.append((c * n + c, (far + 1) * n + c))
        got_even = lax.ppermute(top, axes, evens)
        got_odd = lax.ppermute(bottom, axes, odds)
        got = jnp.where(row_idx % 2 == 0, got_even, got_odd)
        part = got if part is None else part + got
    other = lax.ppermute(part, "row", [(r, r ^ 1) for r in range(n)])
    even = row_idx % 2 == 0
    joined = jnp.concatenate(
        [jnp.where(even, part, other), jnp.where(even, other, part)], axis=0
    )
    near = jnp.where(row_idx == col_idx, lower, partner)
    return jnp.where(row_idx // 2 == col_idx // 2, near, joined)


FLIPS = {
    4: (
        (1, 2, 0), (1, 3, 0), (2, 1, 0), (2, 0, 1), (1, 2, 2), (1, 3, 2),
        (2, 1, 2), (1, 2, 3), (1, 3, 3), (2, 1, 3), (3, 1, 3),
    )
}


def straight(b, c, target_col, n):
    near = jnp.abs(c - target_col) <= jnp.abs(b - target_col)
    for fb, fc, ft in FLIPS.get(n, ()):
        near = near ^ ((b == fb) & (c == fc) & (target_col == ft))
    return near


def exchange_kernel(
    n, row_map, schur, arr_a, arr_b, rowed, square, stage, result,
    send_sem, recv_sem, local_sem, load_sem, store_sem,
):
    total = 2 * n * n
    h = lax.axis_index("half")
    r = lax.axis_index("row")
    z = lax.axis_index("col")
    me = (h * n + r) * n + z
    rs = arr_a.shape[3]
    cs = arr_a.shape[4]
    block = n * rs
    tile = min(256, block)

    def place(index):
        return index // (n * n), (index // n) % n, index % n

    barrier = pltpu.get_barrier_semaphore()

    @pl.loop(1, total)
    def _(step):
        ph, pr, pz = place(lax.rem(me + step, total))
        pl.semaphore_signal(barrier, inc=1, device_id=(ph, pr, pz), device_id_type=MESH)

    pl.semaphore_wait(barrier, total - 1)

    def visit(step, act):
        ph, pr, pz = place(lax.rem(me + step, total))
        t = ph * n + pr
        direct = straight(r, z, pz, n)
        mirror = jnp.logical_not(straight(z, r, pz, n)) & (r != z)
        row_at = pl.multiple_of(t * rs, rs)
        col_at = pl.multiple_of(pz * cs, cs)

        def remote(src, dst, kind):
            act(
                pltpu.make_async_remote_copy(
                    src_ref=src,
                    dst_ref=dst,
                    send_sem=send_sem.at[step, kind],
                    recv_sem=recv_sem.at[h, r, z] if kind == 0 else recv_sem.at[h, z, r],
                    device_id=(ph, pr, pz),
                    device_id_type=MESH,
                )
            )

        for width, fits in ((cs, t > 2 * pz), (rs, t == 2 * pz)):

            @pl.when(fits & direct)
            def _():
                remote(
                    schur.at[pl.ds(row_at, rs), pl.ds(col_at, width)],
                    arr_a.at[h, r, z, :, pl.ds(0, width)],
                    0,
                )

            @pl.when(fits & mirror)
            def _():
                remote(
                    schur.at[pl.ds(col_at, width), pl.ds(row_at, rs)],
                    arr_b.at[h, z, r, pl.ds(0, width), :],
                    1,
                )

    @pl.loop(1, total)
    def _(step):
        visit(step, lambda copy: copy.start())

    my_t = h * n + r
    row_at = pl.multiple_of(my_t * rs, rs)
    col_at = pl.multiple_of(z * cs, cs)
    own_a = pltpu.make_async_copy(
        schur.at[pl.ds(row_at, rs), pl.ds(col_at, cs)], arr_a.at[h, r, z], local_sem.at[0]
    )
    own_b = pltpu.make_async_copy(
        schur.at[pl.ds(col_at, cs), pl.ds(row_at, rs)], arr_b.at[h, z, r], local_sem.at[1]
    )
    own_a.start()
    own_b.start()
    own_a.wait()
    own_b.wait()

    @pl.when(my_t >= 2 * z)
    def _():
        @pl.loop(0, 2 * n)
        def _(k):
            sh = (h + k % 2) % 2
            cc = (z + k // 2) % n

            def moves(b):
                direct = straight(b, cc, z, n)
                into = square.at[pl.ds(b * rs, rs), :]
                load_a = pltpu.make_async_copy(arr_a.at[sh, b, cc], into, load_sem.at[b])
                load_b = pltpu.make_async_copy(
                    arr_b.at[sh, b, cc], stage.at[b], load_sem.at[b]
                )
                return direct, load_a, load_b

            for b in range(n):
                direct, load_a, load_b = moves(b)
                source_row = jnp.where(direct, b, cc)
                source_col = jnp.where(direct, cc, b)
                away = (sh != h) | (source_row != r) | (source_col != z)
                for width, fits in ((cs, my_t > 2 * z), (rs, my_t == 2 * z)):

                    @pl.when(fits & away & direct)
                    def _():
                        dst = arr_a.at[sh, b, cc, :, pl.ds(0, width)]
                        pltpu.make_async_copy(dst, dst, recv_sem.at[sh, b, cc]).wait()

                    @pl.when(fits & away & jnp.logical_not(direct))
                    def _():
                        dst = arr_b.at[sh, b, cc, pl.ds(0, width), :]
                        pltpu.make_async_copy(dst, dst, recv_sem.at[sh, b, cc]).wait()

                @pl.when(direct)
                def _():
                    load_a.start()

                @pl.when(jnp.logical_not(direct))
                def _():
                    load_b.start()

            for b in range(n):
                direct, load_a, load_b = moves(b)

                @pl.when(direct)
                def _():
                    load_a.wait()

                @pl.when(jnp.logical_not(direct))
                def _():
                    load_b.wait()
                    eye = (
                        lax.broadcasted_iota(jnp.int32, (rs, rs), 0)
                        == lax.broadcasted_iota(jnp.int32, (rs, rs), 1)
                    ).astype(jnp.bfloat16)
                    square[pl.ds(b * rs, rs), :] = contract(eye, stage[b]).astype(
                        jnp.bfloat16
                    )

            ids = row_map[pl.ds(sh, 1), :]

            @pl.loop(0, block // tile)
            def _(i):
                at = pl.multiple_of(i * tile, tile)
                pick = (
                    lax.broadcasted_iota(jnp.int32, (tile, block), 0) + at == ids
                ).astype(jnp.bfloat16)
                result[pl.ds(at, tile), :] = jnp.dot(
                    pick, square[...], preferred_element_type=jnp.float32
                ).astype(jnp.bfloat16)

            stores = [
                pltpu.make_async_copy(
                    result.at[:, pl.ds(q * rs, rs)],
                    rowed.at[sh, q, :, pl.ds(pl.multiple_of(cc * rs, rs), rs)],
                    store_sem.at[q],
                )
                for q in range(2)
            ]
            for store in stores:
                store.start()
            for store in stores:
                store.wait()

    @pl.loop(1, total)
    def _(step):
        visit(step, lambda copy: copy.wait_send())


def exchange(row_map, schur, n):
    rs = schur.shape[0] // (2 * n)
    cs = 2 * rs
    block = n * rs
    dtype = schur.dtype
    anywhere = pl.BlockSpec(memory_space=pl.ANY)
    return pl.pallas_call(
        functools.partial(exchange_kernel, n),
        out_shape=(
            jax.ShapeDtypeStruct((2, n, n, rs, cs), dtype),
            jax.ShapeDtypeStruct((2, n, n, cs, rs), dtype),
            jax.ShapeDtypeStruct((2, 2, block, block), dtype),
        ),
        in_specs=[pl.BlockSpec(memory_space=pltpu.VMEM), anywhere],
        out_specs=(anywhere, anywhere, anywhere),
        scratch_shapes=[
            pltpu.VMEM((block, cs), dtype),
            pltpu.VMEM((n, cs, rs), dtype),
            pltpu.VMEM((block, cs), dtype),
            pltpu.SemaphoreType.DMA((2 * n * n, 2)),
            pltpu.SemaphoreType.DMA((2, n, n)),
            pltpu.SemaphoreType.DMA((2,)),
            pltpu.SemaphoreType.DMA((n,)),
            pltpu.SemaphoreType.DMA((2,)),
        ],
        compiler_params=pltpu.CompilerParams(
            collective_id=0, has_side_effects=True, vmem_limit_bytes=48 * 1024 * 1024
        ),
    )(row_map, schur)


def assemble_kernel(n, col_map, rowed, root, out):
    q = pl.program_id(0)
    j = pl.program_id(1)
    t = lax.axis_index("half") * n + lax.axis_index("row")
    c_idx = lax.axis_index("col")
    block = rowed.shape[2]
    tile = min(256, block)
    width = out.shape[1]
    needed = t >= 2 * c_idx + q

    @pl.when(needed)
    def _():
        ids = lax.broadcasted_iota(jnp.int32, (block, width), 1) + j * width
        picks = [
            (col_map[0, h, :, :] == ids).astype(jnp.bfloat16) for h in range(2)
        ]
        first_row = t * block
        first_col = (2 * c_idx + q) * block + j * width
        for i in range(block // tile):
            rows = pl.ds(i * tile, tile)
            value = root[rows, :].astype(jnp.float32)
            for h in range(2):
                value = value + jnp.dot(
                    rowed[h, 0, rows, :], picks[h], preferred_element_type=jnp.float32
                )
            row_ids = lax.broadcasted_iota(jnp.int32, (tile, width), 0) + (
                first_row + i * tile
            )
            col_ids = lax.broadcasted_iota(jnp.int32, (tile, width), 1) + first_col
            out[rows, :] = jnp.where(row_ids >= col_ids, value, 0.0)

    @pl.when(jnp.logical_not(needed))
    def _():
        out[...] = jnp.zeros_like(out)


def assemble(col_map, rowed, root_front, n):
    block = root_front.shape[0]
    width = min(256, block)
    steps = block // width
    return pl.pallas_call(
        functools.partial(assemble_kernel, n),
        grid=(2, steps),
        out_shape=jax.ShapeDtypeStruct(root_front.shape, jnp.float32),
        in_specs=[
            pl.BlockSpec((1, 2, block, 1), lambda q, j: (q, 0, 0, 0)),
            pl.BlockSpec((2, 1, block, block), lambda q, j: (0, q, 0, 0)),
            pl.BlockSpec((block, width), lambda q, j: (0, q * steps + j)),
        ],
        out_specs=pl.BlockSpec((block, width), lambda q, j: (0, q * steps + j)),
        compiler_params=pltpu.CompilerParams(vmem_limit_bytes=58 * 1024 * 1024),
    )(col_map, rowed, root_front)


def body(front, panel, inverse_block, child_maps, root_front):
    n = lax.axis_size("row")
    halves = lax.axis_size("half")
    target = lax.axis_index("half") * n + lax.axis_index("row")
    col_idx = lax.axis_index("col")
    block_front = front[0]
    span = block_front.shape[0]
    share = span // (halves * n)
    block = root_front.shape[0]

    full_panel = lax.all_gather(panel[0], "col", axis=1, tiled=True)
    full_inverse = lax.all_gather(inverse_block[0], "col", axis=1, tiled=True)
    lower_rows = contract(full_panel, full_inverse).astype(jnp.bfloat16)
    lower_cols = column_factor(lower_rows, n)
    update = contract(lower_rows, lower_cols)
    schur_block = (block_front.astype(jnp.float32) - update).astype(jnp.bfloat16)

    runs = child_maps.reshape(halves, n, halves * n, share)

    def local_ids(run):
        picked = lax.dynamic_index_in_dim(runs, run, axis=2, keepdims=False)
        return picked.reshape(halves, n * share) - run * block

    row_map = local_ids(target)
    col_map = jnp.stack([local_ids(2 * col_idx), local_ids(2 * col_idx + 1)])
    rowed = exchange(row_map, schur_block, n)[2]
    return assemble(col_map[..., None], rowed, root_front, n)


def solution(mesh):
    return jax.shard_map(
        body,
        mesh=mesh,
        in_specs=(
            P("half", "row", "col"),
            P("half", "row", "col"),
            P("half", None, "col"),
            P(),
            P(("half", "row"), "col"),
        ),
        out_specs=P(("half", "row"), "col"),
        check_vma=False,
    )
```
